32 devices in a mesh: leaf: 16 (over z, y, x), panel: 2 (over core).
Axes of the slice: x: 2, y: 2, z: 4, core: 2. Of those that a mesh axis runs over, the one named last changes fastest.
Arguments:
- rhs_0: bfloat16 [4096, 256], P('leaf', 'panel'), may hold values from -6 to 6
- rhs_1: bfloat16 [4096, 256], P('leaf', 'panel'), may hold values from -6 to 6
- rhs_2: bfloat16 [4096, 256], P('leaf', 'panel'), may hold values from -6 to 6
- rhs_3: bfloat16 [4096, 256], P('leaf', 'panel'), may hold values from -6 to 6
- inv_0: bfloat16 [4096, 4096], P(('leaf', 'panel')), as said below
- inv_1: bfloat16 [4096, 2048], P(('leaf', 'panel')), as said below
- inv_2: bfloat16 [4096, 1024], P(('leaf', 'panel')), as said below
- inv_3: bfloat16 [4096, 512], P(('leaf', 'panel')), as said below
- coupling_1: bfloat16 [4096, 2048], P(('leaf', 'panel')), may hold values from -0.125 to 0.125
- coupling_2: bfloat16 [4096, 1024], P(('leaf', 'panel')), may hold values from -0.1875 to 0.1875
- coupling_3: bfloat16 [4096, 512], P(('leaf', 'panel')), may hold values from -0.25 to 0.25
- update_rows_1: int32 [2, 2048], replicated, may hold values from 0 to 4095, as said below
- update_rows_2: int32 [4, 1024], replicated, may hold values from 0 to 6143, as said below
- update_rows_3: int32 [8, 512], replicated, may hold values from 0 to 7167, as said below
Outputs:
- solution_0: bfloat16 [4096, 256], P('leaf', 'panel')
- solution_1: bfloat16 [4096, 256], P('leaf', 'panel')
- solution_2: bfloat16 [4096, 256], P('leaf', 'panel')
- solution_3: bfloat16 [4096, 256], P('leaf', 'panel')
The draws below stay inside these ranges and needn't reach their ends.
Inputs may be any that keep to these rules, and one draw needn't show every extreme that they name: `update_rows_1`: row f lists the update rows of front f of depth 1: 2048 distinct indices into its ancestor rows, holding 0 and the last ancestor row. `update_rows_2`: row f lists the update rows of front f of depth 2: 1024 distinct indices into its ancestor rows, holding 0 and the last ancestor row. `update_rows_3`: row f lists the update rows of front f of depth 3: 512 distinct indices into its ancestor rows, holding 0 and the last ancestor row. `inv_0`: the block is lower triangular with its diagonal between 0.5 and 2. `inv_1`: each 2048-row block is lower triangular with its diagonal between 0.5 and 2. `inv_2`: each 1024-row block is lower triangular with its diagonal between 0.5 and 2. `inv_3`: each 512-row block is lower triangular with its diagonal between 0.5 and 2.
All inputs are finite; a program needn't handle non-finite values.
Results may differ from the reference program's by a relative error of at most 0.014.
Values may be sent and summed in bfloat16 or wider, within the bound.
A program may use at most 64 MiB of HBM per device.

```python
import math
import jax
import jax.numpy as jnp

PIVOTS = 4096
LEVELS = 4
RHS = 256


def lower_inverse(key, front_rows):
    noise_draw = jax.random.normal(key, (PIVOTS, front_rows), jnp.float32)
    row_within = jnp.arange(PIVOTS, dtype=jnp.int32) % front_rows
    column_ids = jnp.arange(front_rows, dtype=jnp.int32)
    below = column_ids[None, :] < row_within[:, None]
    on_diagonal = column_ids[None, :] == row_within[:, None]
    diag_key = jax.random.fold_in(key, 7)
    diag_values = jnp.exp(jax.random.uniform(diag_key, (PIVOTS,), jnp.float32, math.log(0.5), math.log(2.0)))
    spread = 0.7
    lower_part = jnp.where(below, noise_draw * (spread / math.sqrt(front_rows)), 0.0)
    values = lower_part + jnp.where(on_diagonal, diag_values[:, None], 0.0)
    return values.astype(jnp.bfloat16)


def draw_inv_0(key, part):
    return lower_inverse(key, PIVOTS)


def draw_inv_1(key, part):
    return lower_inverse(key, PIVOTS // 2)


def draw_inv_2(key, part):
    return lower_inverse(key, PIVOTS // 4)


def draw_inv_3(key, part):
    return lower_inverse(key, PIVOTS // 8)


def ancestor_lists(key, depth_now):
    list_length = PIVOTS >> depth_now
    span_rows = 0
    for upper in range(depth_now):
        span_rows = span_rows + (PIVOTS >> upper)
    row_lists = []
    for front in range(2 ** depth_now):
        node_key = jax.random.fold_in(key, 100 * depth_now + front)
        inner = jax.random.permutation(node_key, span_rows - 2)[:list_length - 2].astype(jnp.int32) + 1
        joined = jnp.concatenate([jnp.zeros((1,), jnp.int32), inner, jnp.full((1,), span_rows - 1, jnp.int32)])
        order_key = jax.random.fold_in(node_key, 11)
        shuffled = jax.random.permutation(order_key, list_length)
        row_lists.append(joined[shuffled])
    return jnp.stack(row_lists).astype(jnp.int32)


def draw_update_rows_1(key, part):
    return ancestor_lists(key, 1)


def draw_update_rows_2(key, part):
    return ancestor_lists(key, 2)


def draw_update_rows_3(key, part):
    return ancestor_lists(key, 3)


def block_scale(stream_key, dims, cuts, smallest, largest):
    def one(position, parts):
        steps = jax.random.uniform(jax.random.fold_in(jax.random.fold_in(stream_key, 6), position), (parts,), jnp.float32, smallest / len(cuts), largest / len(cuts))
        return jnp.repeat(jnp.exp(steps), dims[position] // parts).reshape((-1,) + (1,) * (len(dims) - position - 1))

    factor_of = one(*cuts[0])
    for cut in cuts[1:]:
        factor_of = factor_of * one(*cut)
    return factor_of


def bell_draw(rng, extent, deviation, most, cuts=(), kind=jnp.bfloat16):
    level = block_scale(rng, extent, cuts, -0.22, 0.18) if cuts else 1.0
    values = jax.random.normal(rng, extent, jnp.float32) * deviation * level
    return jnp.minimum(jnp.maximum(values, -most), most).astype(kind)


def setup_inputs(seed: int = 0) -> dict:
    keys = jax.random.split(jax.random.key(seed), 15)
    return {
        "rhs_0": bell_draw(keys[0], (PIVOTS, RHS), 1.0, 6.0, ((0, 16), (1, 2))),
        "rhs_1": bell_draw(keys[1], (PIVOTS, RHS), 1.0, 6.0, ((0, 16), (1, 2))),
        "rhs_2": bell_draw(keys[2], (PIVOTS, RHS), 1.0, 6.0, ((0, 16), (1, 2))),
        "rhs_3": bell_draw(keys[3], (PIVOTS, RHS), 1.0, 6.0, ((0, 16), (1, 2))),
        "inv_0": draw_inv_0(jax.random.fold_in(keys[14], 71), 0),
        "inv_1": draw_inv_1(jax.random.fold_in(keys[14], 71), 0),
        "inv_2": draw_inv_2(jax.random.fold_in(keys[14], 71), 0),
        "inv_3": draw_inv_3(jax.random.fold_in(keys[14], 71), 0),
        "coupling_1": bell_draw(keys[8], (PIVOTS, PIVOTS // 2), (PIVOTS // 2) ** -0.5, 0.125, ((0, 32),)),
        "coupling_2": bell_draw(keys[9], (PIVOTS, PIVOTS // 4), (PIVOTS // 4) ** -0.5, 0.1875, ((0, 32),)),
        "coupling_3": bell_draw(keys[10], (PIVOTS, PIVOTS // 8), (PIVOTS // 8) ** -0.5, 0.25, ((0, 32),)),
        "update_rows_1": draw_update_rows_1(jax.random.fold_in(keys[14], 71), 0),
        "update_rows_2": draw_update_rows_2(jax.random.fold_in(keys[14], 71), 0),
        "update_rows_3": draw_update_rows_3(jax.random.fold_in(keys[14], 71), 0),
    }


def reference(rhs_0, rhs_1, rhs_2, rhs_3, inv_0, inv_1, inv_2, inv_3, coupling_1, coupling_2, coupling_3, update_rows_1, update_rows_2, update_rows_3):
    rhs_all = [rhs_0, rhs_1, rhs_2, rhs_3]
    inv_all = [inv_0, inv_1, inv_2, inv_3]
    coupling_all = [None, coupling_1, coupling_2, coupling_3]
    lists_all = [None, update_rows_1, update_rows_2, update_rows_3]
    columns = rhs_0.shape[1]
    front_sizes = [PIVOTS >> depth_now for depth_now in range(LEVELS)]
    offsets = [0]
    for depth_now in range(1, LEVELS):
        offsets.append(offsets[-1] + front_sizes[depth_now - 1])
    received = [jnp.zeros((PIVOTS, columns), jnp.float32) for upper in range(LEVELS - 1)]
    forwards = [[None] * (2 ** depth_now) for depth_now in range(LEVELS)]
    for depth_now in reversed(range(LEVELS)):
        front_rows = front_sizes[depth_now]
        for front in range(2 ** depth_now):
            row_start = front * front_rows
            summed = rhs_all[depth_now][row_start:row_start + front_rows].astype(jnp.float32)
            if depth_now < LEVELS - 1:
                summed = summed + received[depth_now][row_start:row_start + front_rows]
            combined = summed.astype(jnp.bfloat16)
            values = jnp.dot(inv_all[depth_now][row_start:row_start + front_rows], combined, preferred_element_type=jnp.float32).astype(jnp.bfloat16)
            forwards[depth_now][front] = values
            if depth_now > 0:
                block = coupling_all[depth_now][row_start:row_start + front_rows]
                update = jnp.dot(block.T, values, preferred_element_type=jnp.float32)
                row_list = lists_all[depth_now][front]
                chain = jnp.zeros((offsets[depth_now], columns), jnp.float32).at[row_list].add(update)
                for upper in range(depth_now):
                    owner = front >> (depth_now - upper)
                    upper_rows = front_sizes[upper]
                    received[upper] = received[upper].at[owner * upper_rows:(owner + 1) * upper_rows].add(chain[offsets[upper]:offsets[upper] + upper_rows])
    solved_all = [[None] * (2 ** depth_now) for depth_now in range(LEVELS)]
    for depth_now in range(LEVELS):
        front_rows = front_sizes[depth_now]
        for front in range(2 ** depth_now):
            row_start = front * front_rows
            values = forwards[depth_now][front]
            if depth_now > 0:
                anc_values = jnp.concatenate([solved_all[upper][front >> (depth_now - upper)] for upper in range(depth_now)], axis=0)
                row_list = lists_all[depth_now][front]
                picked = jnp.take(anc_values, row_list, axis=0)
                block = coupling_all[depth_now][row_start:row_start + front_rows]
                pulled = jnp.dot(block, picked, preferred_element_type=jnp.float32)
                adjusted = (values.astype(jnp.float32) - pulled).astype(jnp.bfloat16)
            else:
                adjusted = values
            inverse = inv_all[depth_now][row_start:row_start + front_rows]
            solved_all[depth_now][front] = jnp.dot(inverse.T, adjusted, preferred_element_type=jnp.float32).astype(jnp.bfloat16)
    outputs = [jnp.concatenate(solved_all[depth_now], axis=0) for depth_now in range(LEVELS)]
    return (outputs[0], outputs[1], outputs[2], outputs[3])
```

```python
import functools

import jax
import jax.numpy as jnp
from jax import lax
from jax.experimental import pallas as pl
from jax.experimental.pallas import tpu as pltpu
from jax.sharding import PartitionSpec as P

LEVELS = 4
MESH = pl.DeviceIdType.MESH


def split_group(groups):
    high = 1
    low = groups
    while low > 8 or (high > 1 and low > 4 and high < 4):
        low //= 2
        high *= 2
    if high > 1 and high < low:
        low, high = low // 2, high * 2
    return low, high


def exchange_kernel(groups, reduce, gather, has_extra, *refs):
    refs = list(refs)
    part_ref = refs.pop(0) if reduce else None
    extra_ref = refs.pop(0) if has_extra else None
    own_ref = refs.pop(0)
    full_ref = refs.pop(0) if gather else None
    if reduce:
        low_buf, high_buf, high_out, rs_send, rs_recv, rz_send, rz_recv = refs[:7]
        refs = refs[7:]
    if gather:
        ag_send, ag_recv, az_send, az_recv = refs[:4]
    low, high = split_group(groups)
    rows = own_ref.shape[0]
    me = lax.axis_index("leaf")
    panel = lax.axis_index("panel")
    base = me // groups * groups
    mine = me - base
    my_low = lax.rem(mine, low)
    my_high = mine // low

    def leaf_of(high_part, low_part):
        return base + high_part * low + low_part

    def low_peer(step):
        return leaf_of(my_high, my_low ^ step)

    def high_peer(step):
        return leaf_of(my_high ^ step, my_low)

    def block(ref, high_part, low_part):
        start = (high_part * low + low_part) * rows
        return ref.at[pl.ds(pl.multiple_of(start, rows), rows)]

    def remote(src, dst, send, recv, leaf):
        return pltpu.make_async_remote_copy(
            src_ref=src, dst_ref=dst, send_sem=send, recv_sem=recv,
            device_id=(leaf, panel), device_id_type=MESH,
        )

    barrier = pltpu.get_barrier_semaphore()
    for step in range(1, low):
        pl.semaphore_signal(barrier, inc=1, device_id=(low_peer(step), panel), device_id_type=MESH)
    for step in range(1, high):
        pl.semaphore_signal(barrier, inc=1, device_id=(high_peer(step), panel), device_id_type=MESH)
    pl.semaphore_wait(barrier, low + high - 2)

    pending = []
    order = list(range(high - 1, 0, -1)) + [0]
    if reduce:
        low_copies = {}
        for plane in order:
            for step in range(low - 1, 0, -1):
                copy = remote(
                    block(part_ref, my_high ^ plane, my_low ^ step),
                    low_buf.at[plane, step - 1],
                    rs_send.at[plane, step - 1], rs_recv.at[plane, step - 1],
                    low_peer(step),
                )
                copy.start()
                low_copies[plane, step] = copy
        high_copies = {}
        for plane in order:
            total = block(part_ref, my_high ^ plane, my_low)[...].astype(jnp.float32)
            if plane == 0 and has_extra:
                total = total + extra_ref[...].astype(jnp.float32)
            for step in range(1, low):
                low_copies[plane, step].wait_recv()
                total = total + low_buf[plane, step - 1].astype(jnp.float32)
            if plane:
                high_out[plane - 1] = total.astype(jnp.bfloat16)
                copy = remote(
                    high_out.at[plane - 1], high_buf.at[plane - 1],
                    rz_send.at[plane - 1], rz_recv.at[plane - 1],
                    high_peer(plane),
                )
                copy.start()
                high_copies[plane] = copy
        for plane in range(1, high):
            high_copies[plane].wait_recv()
            total = total + high_buf[plane - 1].astype(jnp.float32)
        own_ref[...] = total.astype(jnp.bfloat16)
        pending += list(low_copies.values()) + list(high_copies.values())
    else:
        own_ref[...] = extra_ref[...]
    if gather:
        block(full_ref, my_high, my_low)[...] = own_ref[...]
        arriving = {}
        for plane in order[:-1]:
            copy = remote(
                own_ref, block(full_ref, my_high, my_low),
                az_send.at[plane - 1], az_recv.at[plane - 1], high_peer(plane),
            )
            copy.start()
            pending.append(copy)
            arriving[plane] = copy
        forwards = []
        for plane in range(high):
            if plane:
                arriving[plane].wait_recv()
            for step in range(low - 1, 0, -1):
                here = block(full_ref, my_high ^ plane, my_low)
                copy = remote(
                    here if plane else own_ref, here,
                    ag_send.at[plane, step - 1], ag_recv.at[plane, step - 1], low_peer(step),
                )
                copy.start()
                pending.append(copy)
                forwards.append(copy)
        for copy in forwards:
            copy.wait_recv()
    for copy in pending:
        copy.wait_send()


def exchange(groups, part, extra, gather, ident):
    reduce = part is not None
    low, high = split_group(groups)
    if reduce:
        rows, columns = part.shape[0] // groups, part.shape[1]
    else:
        rows, columns = extra.shape
    own = jax.ShapeDtypeStruct((rows, columns), jnp.bfloat16)
    full = jax.ShapeDtypeStruct((rows * groups, columns), jnp.bfloat16)
    highs = max(high - 1, 1)
    dma = pltpu.SemaphoreType.DMA
    scratch = []
    if reduce:
        scratch += [
            pltpu.VMEM((high, low - 1, rows, columns), jnp.bfloat16),
            pltpu.VMEM((highs, rows, columns), jnp.bfloat16),
            pltpu.VMEM((highs, rows, columns), jnp.bfloat16),
            dma((high, low - 1)), dma((high, low - 1)), dma((highs,)), dma((highs,)),
        ]
    if gather:
        scratch += [dma((high, low - 1)), dma((high, low - 1)), dma((highs,)), dma((highs,))]
    operands = [value for value in (part, extra) if value is not None]
    outs = (own, full) if gather else (own,)
    vmem = pl.BlockSpec(memory_space=pltpu.VMEM)
    return pl.pallas_call(
        functools.partial(exchange_kernel, groups, reduce, gather, extra is not None),
        out_shape=outs,
        in_specs=[vmem] * len(operands),
        out_specs=tuple([vmem] * len(outs)),
        scratch_shapes=scratch,
        compiler_params=pltpu.CompilerParams(
            collective_id=ident, has_side_effects=True, vmem_limit_bytes=32 * 2**20
        ),
    )(*operands)


def contract_rows(left, right):
    return lax.dot_general(
        left, right, (((0,), (0,)), ((), ())), preferred_element_type=jnp.float32
    )


def body(
    rhs_0, rhs_1, rhs_2, rhs_3,
    inv_0, inv_1, inv_2, inv_3,
    coupling_1, coupling_2, coupling_3,
    update_rows_1, update_rows_2, update_rows_3,
):
    rhs_all = [rhs_0, rhs_1, rhs_2, rhs_3]
    lists_all = [None, update_rows_1, update_rows_2, update_rows_3]
    columns = rhs_0.shape[1]
    leaf_count = lax.axis_size("leaf")
    front_sizes = [inv_0.shape[1], inv_1.shape[1], inv_2.shape[1], inv_3.shape[1]]
    offsets = [0]
    for depth_now in range(1, LEVELS):
        offsets.append(offsets[-1] + front_sizes[depth_now - 1])

    def whole_rows(value):
        return lax.all_gather(value, "panel", axis=0, tiled=True)

    inv_3, coupling_3 = whole_rows(inv_3), whole_rows(coupling_3)
    inv_2, coupling_2 = whole_rows(inv_2), whole_rows(coupling_2)
    inv_1, coupling_1 = whole_rows(inv_1), whole_rows(coupling_1)
    inv_all = [whole_rows(inv_0), inv_1, inv_2, inv_3]
    coup_all = [None, coupling_1, coupling_2, coupling_3]
    accumulated = jnp.zeros((offsets[LEVELS - 1], columns), jnp.float32)
    forwards = [None] * LEVELS
    row_lists = [None] * LEVELS
    for depth_now in reversed(range(LEVELS)):
        groups = leaf_count >> depth_now
        front_rows = front_sizes[depth_now]
        front = lax.axis_index("leaf") // groups
        part = None
        if depth_now < LEVELS - 1:
            start = offsets[depth_now]
            part = accumulated[start : start + front_rows].astype(jnp.bfloat16)
        _, combined = exchange(groups, part, rhs_all[depth_now], True, depth_now)
        values = jnp.dot(
            inv_all[depth_now], combined, preferred_element_type=jnp.float32
        ).astype(jnp.bfloat16)
        forwards[depth_now] = values
        if depth_now > 0:
            update = contract_rows(coup_all[depth_now], values)
            row_lists[depth_now] = lax.dynamic_index_in_dim(
                lists_all[depth_now], front, 0, keepdims=False
            )
            accumulated = accumulated.at[row_lists[depth_now]].add(update)
    anc_values = []
    outputs = []
    for depth_now in range(LEVELS):
        groups = leaf_count >> depth_now
        adjusted = forwards[depth_now]
        if depth_now > 0:
            picked = jnp.take(jnp.concatenate(anc_values, axis=0), row_lists[depth_now], axis=0)
            pulled = jnp.dot(coup_all[depth_now], picked, preferred_element_type=jnp.float32)
            adjusted = (adjusted.astype(jnp.float32) - pulled).astype(jnp.bfloat16)
        partial_value = contract_rows(inv_all[depth_now], adjusted).astype(jnp.bfloat16)
        last = depth_now == LEVELS - 1
        found = exchange(groups, partial_value, None, not last, LEVELS + depth_now)
        outputs.append(found[0])
        if not last:
            anc_values.append(found[1])
    return tuple(outputs)


def solution(mesh):
    in_specs = (P("leaf", "panel"),) * 4 + (P(("leaf", "panel"), None),) * 7 + (P(),) * 3
    out_specs = (P("leaf", "panel"),) * 4
    return jax.shard_map(body, mesh=mesh, in_specs=in_specs, out_specs=out_specs, check_vma=False)
```

```python
import functools

import jax
import jax.numpy as jnp
from jax import lax
from jax.experimental import pallas as pl
from jax.experimental.pallas import tpu as pltpu
from jax.sharding import PartitionSpec as P

LEVELS = 4
MESH = pl.DeviceIdType.MESH
BF16 = jnp.bfloat16
F32 = jnp.float32


def split_group(groups):
    low, high = groups, 1
    while low > 8 or (high > 1 and low > 4 and high < 4):
        low, high = low // 2, high * 2
    return low, high


def contract_rows(left, right):
    return lax.dot_general(left, right, (((0,), (0,)), ((), ())), preferred_element_type=F32)


def kernel(leaf_count, panel_count, *refs):
    refs = list(refs)

    def take(count):
        taken = refs[:count]
        del refs[:count]
        return taken

    rhs = take(LEVELS)
    inv_in = take(LEVELS)
    coup_in = [None] + take(LEVELS - 1)
    list_rows, list_cols = take(2)
    outs = take(LEVELS)
    inv = take(LEVELS)
    coup = [None] + take(LEVELS - 1)
    forwards = take(LEVELS)
    updates, picked = take(2)
    factor_local, factor_send, factor_recv = take(3)
    levels_forward = [None] * LEVELS
    levels_backward = [None] * LEVELS
    for depth in range(LEVELS):
        levels_forward[depth] = (take(9) if depth < LEVELS - 1 else None, take(5))
        levels_backward[depth] = (take(9), take(5) if depth < LEVELS - 1 else None)

    me = lax.axis_index("leaf")
    panel = lax.axis_index("panel")
    rows, columns = rhs[0].shape
    factor_rows = inv_in[0].shape[0]
    sizes = [ref.shape[1] for ref in inv_in]
    offsets = [sum(sizes[:depth]) for depth in range(LEVELS)]
    places = [None] + [sum(sizes[1:depth]) for depth in range(1, LEVELS + 1)]
    chunk = list_rows.shape[1]
    streamed = rows % 128 == 0
    merged = factor_rows % 16 == 0

    masks = set()
    for depth in range(LEVELS):
        low, high = split_group(leaf_count >> depth)
        masks |= set(range(1, low)) | set(low * plane for plane in range(1, high))
    barrier = pltpu.get_barrier_semaphore()
    for mask in sorted(masks):
        pl.semaphore_signal(barrier, inc=1, device_id=(me ^ mask, panel), device_id_type=MESH)
    for shift in range(1, panel_count):
        pl.semaphore_signal(
            barrier, inc=1, device_id=(me, lax.rem(panel + shift, panel_count)), device_id_type=MESH
        )

    def local_factor(source, target, slot):
        return pltpu.make_async_copy(source, target.at[panel], factor_local.at[slot])

    def remote_factor(source, target, slot, shift):
        return pltpu.make_async_remote_copy(
            src_ref=source, dst_ref=target.at[panel],
            send_sem=factor_send.at[slot, shift - 1], recv_sem=factor_recv.at[slot, shift - 1],
            device_id=(me, lax.rem(panel + shift, panel_count)), device_id_type=MESH,
        )

    factors = []
    for depth in reversed(range(LEVELS)):
        factors.append((inv_in[depth], inv[depth], depth))
        if depth:
            factors.append((coup_in[depth], coup[depth], LEVELS + depth))
    for factor in factors:
        local_factor(*factor).start()
    pl.semaphore_wait(barrier, len(masks) + panel_count - 1)
    for factor in factors:
        for shift in range(1, panel_count):
            remote_factor(*factor, shift).start()

    def wait_factor(slot):
        for factor in factors:
            if factor[2] == slot:
                local_factor(*factor).wait()
                for shift in range(1, panel_count):
                    remote_factor(*factor, shift).wait_recv()

    def row_parts(ref, start, size):
        if merged:
            value = ref[:, :, pl.ds(start, size)]
            return [value.reshape(panel_count * factor_rows, size)]
        return [ref[index, :, pl.ds(start, size)] for index in range(panel_count)]

    def contracted(ref, start, size, values):
        total = None
        for index, part in enumerate(row_parts(ref, start, size)):
            term = contract_rows(part, values[index])
            total = term if total is None else total + term
        return total

    def read_values(ref):
        if merged:
            return [ref[...].reshape(panel_count * factor_rows, columns)]
        return [ref[index] for index in range(panel_count)]

    def write_values(ref, values):
        if merged:
            ref[...] = values[0].reshape(panel_count, factor_rows, columns)
        else:
            for index in range(panel_count):
                ref[index] = values[index]

    def block_of(ref, index):
        return ref.at[pl.ds(pl.multiple_of(index * rows, rows), rows)]

    def remote(source, target, send, recv, mask):
        return pltpu.make_async_remote_copy(
            src_ref=source, dst_ref=target, send_sem=send, recv_sem=recv,
            device_id=(me ^ mask, panel), device_id_type=MESH,
        )

    late = []

    def reduce_blocks(depth, buffers, block_value):
        part, kept, low_buf, high_out, high_buf, low_send, low_recv, high_send, high_recv = buffers
        groups = leaf_count >> depth
        mine = lax.rem(me, groups)
        low, high = split_group(groups)

        def low_copy(plane, step):
            return remote(
                block_of(part, mine ^ (plane * low + step)), low_buf.at[plane, step - 1],
                low_send.at[plane, step - 1], low_recv.at[plane, step - 1], step,
            )

        def issue(plane):
            def one(count, carry):
                step = low - 1 - count
                index = mine ^ (plane * low + step)
                block_of(part, index)[...] = block_value(index).astype(BF16)
                low_copy(plane, step).start()
                return carry

            lax.fori_loop(0, low - 1, one, 0)
            kept[plane] = block_value(mine ^ (plane * low))

        def high_copy(plane):
            return remote(
                high_out.at[plane - 1], high_buf.at[plane - 1],
                high_send.at[plane - 1], high_recv.at[plane - 1], plane * low,
            )

        def plane_sum(plane):
            total = kept[plane]
            for step in range(1, low):
                low_copy(plane, step).wait_recv()
                late.append(low_copy(plane, step))
                total = total + low_buf[plane, step - 1].astype(F32)
            return total

        issue(high - 1)
        for plane in range(high - 1, 0, -1):
            issue(plane - 1)
            high_out[plane - 1] = plane_sum(plane).astype(BF16)
            high_copy(plane).start()
            late.append(high_copy(plane))
        total = plane_sum(0)
        for plane in range(1, high):
            high_copy(plane).wait_recv()
            total = total + high_buf[plane - 1].astype(F32)
        return total

    def gather_blocks(depth, buffers, use):
        full, low_send, low_recv, high_send, high_recv = buffers
        groups = leaf_count >> depth
        mine = lax.rem(me, groups)
        low, high = split_group(groups)

        def low_copy(plane, step):
            here = block_of(full, mine ^ (plane * low))
            return remote(
                here, here, low_send.at[plane, step - 1], low_recv.at[plane, step - 1], step
            )

        def high_copy(plane):
            here = block_of(full, mine)
            return remote(
                here, here, high_send.at[plane - 1], high_recv.at[plane - 1], plane * low
            )

        def use_low(plane):
            for step in range(1, low):
                low_copy(plane, step).wait_recv()
                use(mine ^ (plane * low + step))

        for plane in range(high - 1, 0, -1):
            high_copy(plane).start()
            late.append(high_copy(plane))
        for plane in range(high):
            if plane:
                high_copy(plane).wait_recv()
            for step in range(low - 1, 0, -1):
                low_copy(plane, step).start()
                late.append(low_copy(plane, step))
            use(mine ^ (plane * low))
            if plane:
                use_low(plane - 1)
        use_low(high - 1)

    def aligned(start):
        return pl.multiple_of(start, rows)

    for depth in reversed(range(LEVELS)):
        groups = leaf_count >> depth
        mine = lax.rem(me, groups)
        reducing, gathering = levels_forward[depth]
        full = gathering[0]
        if reducing is not None:
            first_chunk = places[depth + 1] // chunk

            def scattered(index, depth=depth, first_chunk=first_chunk):
                base = offsets[depth] + index * rows
                row_ids = lax.broadcasted_iota(jnp.int32, (rows, chunk), 0) + base

                def one(step, total):
                    ones = jnp.where(list_rows[pl.ds(step, 1), :] == row_ids, 1.0, 0.0)
                    start = pl.multiple_of(step * chunk, chunk)
                    values = updates[pl.ds(start, chunk), :]
                    return total + jnp.dot(ones.astype(BF16), values, preferred_element_type=F32)

                return lax.fori_loop(
                    first_chunk, list_rows.shape[0], one, jnp.zeros((rows, columns), F32)
                )

            total = reduce_blocks(depth, reducing, scattered)
            combined = (total + rhs[depth][...].astype(F32)).astype(BF16)
        else:
            combined = rhs[depth][...]
        block_of(full, mine)[...] = combined
        sums = [None]
        ready = [False]

        def multiply(index, depth=depth, full=full, sums=sums, ready=ready):
            if not streamed:
                return
            if not ready[0]:
                wait_factor(depth)
                ready[0] = True
            part = row_parts(inv[depth], aligned(index * rows), rows)
            block = block_of(full, index)[...]
            terms = [jnp.dot(value, block, preferred_element_type=F32) for value in part]
            old = sums[0]
            sums[0] = terms if old is None else [a + b for a, b in zip(old, terms)]

        gather_blocks(depth, gathering, multiply)
        if not streamed:
            wait_factor(depth)
            part = row_parts(inv[depth], 0, sizes[depth])
            sums[0] = [jnp.dot(value, full[...], preferred_element_type=F32) for value in part]
        values = [value.astype(BF16) for value in sums[0]]
        write_values(forwards[depth], values)
        if depth:
            wait_factor(LEVELS + depth)

            def update_chunk(step, carry, depth=depth, values=values):
                start = pl.multiple_of(step * chunk, chunk)
                place = pl.multiple_of(places[depth] + step * chunk, chunk)
                values = read_values(forwards[depth])
                updates[pl.ds(place, chunk), :] = contracted(
                    coup[depth], start, chunk, values
                ).astype(BF16)
                return carry

            lax.fori_loop(0, sizes[depth] // chunk, update_chunk, 0)

    picked[...] = jnp.zeros_like(picked)
    for depth in range(LEVELS):
        groups = leaf_count >> depth
        mine = lax.rem(me, groups)
        reducing, gathering = levels_backward[depth]
        if depth:
            def pull(step, totals, depth=depth):
                start = pl.multiple_of(step * chunk, chunk)
                place = pl.multiple_of(places[depth] + step * chunk, chunk)
                part = row_parts(coup[depth], start, chunk)
                rows_now = picked[pl.ds(place, chunk), :].astype(BF16)
                return [
                    total - jnp.dot(value, rows_now, preferred_element_type=F32)
                    for total, value in zip(totals, part)
                ]

            totals = [value.astype(F32) for value in read_values(forwards[depth])]
            totals = lax.fori_loop(0, sizes[depth] // chunk, pull, totals)
            write_values(forwards[depth], [value.astype(BF16) for value in totals])

        if streamed:
            def product(index, depth=depth):
                values = read_values(forwards[depth])
                return contracted(inv[depth], aligned(index * rows), rows, values)
        else:
            whole_product = reducing[0]
            values = read_values(forwards[depth])
            whole_product[...] = contracted(inv[depth], 0, sizes[depth], values).astype(BF16)

            def product(index, whole_product=whole_product):
                return block_of(whole_product, index)[...].astype(F32)

        solved = reduce_blocks(depth, reducing, product).astype(BF16)
        outs[depth][...] = solved
        if gathering is not None:
            full = gathering[0]
            block_of(full, mine)[...] = solved
            first_chunk = places[depth + 1] // chunk

            def pick(index, depth=depth, full=full, first_chunk=first_chunk):
                base = offsets[depth] + index * rows
                row_ids = lax.broadcasted_iota(jnp.int32, (chunk, rows), 1) + base
                block = block_of(full, index)[...]

                def one(step, carry):
                    start = pl.multiple_of(step * chunk, chunk)
                    here = pl.ds(start, chunk)
                    ones = jnp.where(list_cols[here, :] == row_ids, 1.0, 0.0).astype(BF16)
                    picked[here, :] += jnp.dot(ones, block, preferred_element_type=F32)
                    return carry

                lax.fori_loop(first_chunk, list_rows.shape[0], one, 0)

            gather_blocks(depth, gathering, pick)

    for copy in late:
        copy.wait_send()
    for factor in factors:
        for shift in range(1, panel_count):
            remote_factor(*factor, shift).wait_send()


def body(*args):
    rhs, inv, coup, lists = args[:4], args[4:8], args[8:11], args[11:]
    rows, columns = rhs[0].shape
    leaf_count = lax.axis_size("leaf")
    panel_count = lax.axis_size("panel")
    factor_rows = inv[0].shape[0]
    sizes = [value.shape[1] for value in inv]
    chunk = sizes[-1]
    leaf = lax.axis_index("leaf")
    chosen = []
    for depth in range(1, LEVELS):
        front = leaf // (leaf_count >> depth)
        chosen.append(lax.dynamic_index_in_dim(lists[depth - 1], front, 0, keepdims=False))
    joined = jnp.concatenate(chosen)
    list_rows = joined.reshape(-1, chunk)
    list_cols = joined.reshape(-1, 1)
    dma = pltpu.SemaphoreType.DMA
    vmem = pltpu.VMEM
    scratch = [vmem((panel_count, factor_rows, size), BF16) for size in sizes]
    scratch += [vmem((panel_count, factor_rows, size), BF16) for size in sizes[1:]]
    scratch += [vmem((panel_count, factor_rows, columns), BF16) for _ in sizes]
    scratch += [vmem((joined.shape[0], columns), BF16), vmem((joined.shape[0], columns), F32)]
    peers = max(panel_count - 1, 1)
    scratch += [dma((2 * LEVELS,)), dma((2 * LEVELS, peers)), dma((2 * LEVELS, peers))]

    def reduce_scratch(depth):
        low, high = split_group(leaf_count >> depth)
        highs = max(high - 1, 1)
        lows = max(low - 1, 1)
        return [
            vmem((sizes[depth], columns), BF16),
            vmem((high, rows, columns), F32),
            vmem((high, lows, rows, columns), BF16),
            vmem((highs, rows, columns), BF16),
            vmem((highs, rows, columns), BF16),
            dma((high, lows)), dma((high, lows)), dma((highs,)), dma((highs,)),
        ]

    def gather_scratch(depth):
        low, high = split_group(leaf_count >> depth)
        highs = max(high - 1, 1)
        lows = max(low - 1, 1)
        return [
            vmem((sizes[depth], columns), BF16),
            dma((high, lows)), dma((high, lows)), dma((highs,)), dma((highs,)),
        ]

    for depth in range(LEVELS):
        if depth < LEVELS - 1:
            scratch += reduce_scratch(depth)
        scratch += gather_scratch(depth)
        scratch += reduce_scratch(depth)
        if depth < LEVELS - 1:
            scratch += gather_scratch(depth)

    in_vmem = pl.BlockSpec(memory_space=vmem)
    anywhere = pl.BlockSpec(memory_space=pl.ANY)
    own = jax.ShapeDtypeStruct((rows, columns), BF16)
    return pl.pallas_call(
        functools.partial(kernel, leaf_count, panel_count),
        out_shape=(own,) * LEVELS,
        in_specs=[in_vmem] * LEVELS + [anywhere] * (2 * LEVELS - 1) + [in_vmem] * 2,
        out_specs=(in_vmem,) * LEVELS,
        scratch_shapes=scratch,
        compiler_params=pltpu.CompilerParams(
            collective_id=0, has_side_effects=True, vmem_limit_bytes=48 * 2**20
        ),
    )(*rhs, *inv, *coup, list_rows, list_cols)


def solution(mesh):
    in_specs = (P("leaf", "panel"),) * 4 + (P(("leaf", "panel"), None),) * 7 + (P(),) * 3
    out_specs = (P("leaf", "panel"),) * 4
    return jax.shard_map(body, mesh=mesh, in_specs=in_specs, out_specs=out_specs, check_vma=False)
```

```python
import functools

import jax
import jax.numpy as jnp
from jax import lax
from jax.experimental import pallas as pl
from jax.experimental.pallas import tpu as pltpu
from jax.sharding import PartitionSpec as P

LEVELS = 4
MESH = pl.DeviceIdType.MESH
BF16 = jnp.bfloat16
F32 = jnp.float32


def split_group(groups):
    low, high = groups, 1
    while low > 8 or (high > 1 and low > 4 and high < 4):
        low, high = low // 2, high * 2
    return low, high


def contract_rows(left, right):
    return lax.dot_general(left, right, (((0,), (0,)), ((), ())), preferred_element_type=F32)


def kernel(leaf_count, panel_count, *refs):
    refs = list(refs)

    def take(count):
        taken = refs[:count]
        del refs[:count]
        return taken

    rhs = take(LEVELS)
    inv_in = take(LEVELS)
    coup_in = [None] + take(LEVELS - 1)
    list_rows, list_cols = take(2)
    outs = take(LEVELS)
    inv = take(LEVELS)
    coup = [None] + take(LEVELS - 1)
    forwards = take(LEVELS)
    updates, picked = take(2)
    factor_local, factor_send, factor_recv = take(3)
    levels_forward = [None] * LEVELS
    levels_backward = [None] * LEVELS
    for depth in range(LEVELS):
        levels_forward[depth] = (take(9) if depth < LEVELS - 1 else None, take(5))
        levels_backward[depth] = (take(9), take(5) if depth < LEVELS - 1 else None)

    me = lax.axis_index("leaf")
    panel = lax.axis_index("panel")
    rows, columns = rhs[0].shape
    factor_rows = inv_in[0].shape[0]
    sizes = [ref.shape[1] for ref in inv_in]
    offsets = [sum(sizes[:depth]) for depth in range(LEVELS)]
    places = [None] + [sum(sizes[1:depth]) for depth in range(1, LEVELS + 1)]
    chunk = list_rows.shape[1]
    streamed = rows % 128 == 0
    merged = factor_rows % 16 == 0

    masks = set()
    for depth in range(LEVELS):
        low, high = split_group(leaf_count >> depth)
        masks |= set(range(1, low)) | set(low * plane for plane in range(1, high))
    barrier = pltpu.get_barrier_semaphore()
    for mask in sorted(masks):
        pl.semaphore_signal(barrier, inc=1, device_id=(me ^ mask, panel), device_id_type=MESH)
    for shift in range(1, panel_count):
        pl.semaphore_signal(
            barrier, inc=1, device_id=(me, lax.rem(panel + shift, panel_count)), device_id_type=MESH
        )

    def local_factor(source, target, slot):
        return pltpu.make_async_copy(source, target.at[panel], factor_local.at[slot])

    def remote_factor(source, target, slot, shift):
        return pltpu.make_async_remote_copy(
            src_ref=source, dst_ref=target.at[panel],
            send_sem=factor_send.at[slot, shift - 1], recv_sem=factor_recv.at[slot, shift - 1],
            device_id=(me, lax.rem(panel + shift, panel_count)), device_id_type=MESH,
        )

    factors = []
    for depth in reversed(range(LEVELS)):
        factors.append((inv_in[depth], inv[depth], depth))
        if depth:
            factors.append((coup_in[depth], coup[depth], LEVELS + depth))
    for factor in factors:
        local_factor(*factor).start()
    pl.semaphore_wait(barrier, len(masks) + panel_count - 1)
    for factor in factors:
        for shift in range(1, panel_count):
            remote_factor(*factor, shift).start()

    def wait_factor(slot):
        for factor in factors:
            if factor[2] == slot:
                local_factor(*factor).wait()
                for shift in range(1, panel_count):
                    remote_factor(*factor, shift).wait_recv()

    def row_parts(ref, start, size):
        if merged:
            value = ref[:, :, pl.ds(start, size)]
            return [value.reshape(panel_count * factor_rows, size)]
        return [ref[index, :, pl.ds(start, size)] for index in range(panel_count)]

    def contracted(ref, start, size, values):
        total = None
        for index, part in enumerate(row_parts(ref, start, size)):
            term = contract_rows(part, values[index])
            total = term if total is None else total + term
        return total

    def read_values(ref):
        if merged:
            return [ref[...].reshape(panel_count * factor_rows, columns)]
        return [ref[index] for index in range(panel_count)]

    def write_values(ref, values):
        if merged:
            ref[...] = values[0].reshape(panel_count, factor_rows, columns)
        else:
            for index in range(panel_count):
                ref[index] = values[index]

    def block_of(ref, index):
        return ref.at[pl.ds(pl.multiple_of(index * rows, rows), rows)]

    def remote(source, target, send, recv, mask):
        return pltpu.make_async_remote_copy(
            src_ref=source, dst_ref=target, send_sem=send, recv_sem=recv,
            device_id=(me ^ mask, panel), device_id_type=MESH,
        )

    late = []

    def reduce_blocks(depth, buffers, block_value):
        part, kept, low_buf, high_out, high_buf, low_send, low_recv, high_send, high_recv = buffers
        groups = leaf_count >> depth
        mine = lax.rem(me, groups)
        low, high = split_group(groups)

        def low_copy(plane, step):
            return remote(
                block_of(part, mine ^ (plane * low + step)), low_buf.at[plane, step - 1],
                low_send.at[plane, step - 1], low_recv.at[plane, step - 1], step,
            )

        def issue(plane):
            def one(count, carry):
                step = low - 1 - count
                index = mine ^ (plane * low + step)
                block_of(part, index)[...] = block_value(index).astype(BF16)
                low_copy(plane, step).start()
                return carry

            lax.fori_loop(0, low - 1, one, 0)
            kept[plane] = block_value(mine ^ (plane * low))

        def high_copy(plane):
            return remote(
                high_out.at[plane - 1], high_buf.at[plane - 1],
                high_send.at[plane - 1], high_recv.at[plane - 1], plane * low,
            )

        def plane_sum(plane):
            total = kept[plane]
            for step in range(1, low):
                low_copy(plane, step).wait_recv()
                late.append(low_copy(plane, step))
                total = total + low_buf[plane, step - 1].astype(F32)
            return total

        issue(high - 1)
        for plane in range(high - 1, 0, -1):
            issue(plane - 1)
            high_out[plane - 1] = plane_sum(plane).astype(BF16)
            high_copy(plane).start()
            late.append(high_copy(plane))
        total = plane_sum(0)
        for plane in range(1, high):
            high_copy(plane).wait_recv()
            total = total + high_buf[plane - 1].astype(F32)
        return total

    def gather_blocks(depth, buffers, use):
        full, low_send, low_recv, high_send, high_recv = buffers
        groups = leaf_count >> depth
        mine = lax.rem(me, groups)
        low, high = split_group(groups)

        def low_copy(plane, step):
            here = block_of(full, mine ^ (plane * low))
            return remote(
                here, here, low_send.at[plane, step - 1], low_recv.at[plane, step - 1], step
            )

        def high_copy(plane):
            here = block_of(full, mine)
            return remote(
                here, here, high_send.at[plane - 1], high_recv.at[plane - 1], plane * low
            )

        def use_low(plane):
            for step in range(1, low):
                low_copy(plane, step).wait_recv()
                use(mine ^ (plane * low + step))

        for plane in range(high - 1, 0, -1):
            high_copy(plane).start()
            late.append(high_copy(plane))
        for plane in range(high):
            if plane:
                high_copy(plane).wait_recv()
            for step in range(low - 1, 0, -1):
                low_copy(plane, step).start()
                late.append(low_copy(plane, step))
            use(mine ^ (plane * low))
            if plane:
                use_low(plane - 1)
        use_low(high - 1)

    def aligned(start):
        return pl.multiple_of(start, rows)

    for depth in reversed(range(LEVELS)):
        groups = leaf_count >> depth
        mine = lax.rem(me, groups)
        reducing, gathering = levels_forward[depth]
        full = gathering[0]
        if reducing is not None:
            first_chunk = places[depth + 1] // chunk

            def scattered(index, depth=depth, first_chunk=first_chunk):
                base = offsets[depth] + index * rows
                row_ids = lax.broadcasted_iota(jnp.int32, (rows, chunk), 0) + base

                def one(step, total):
                    ones = jnp.where(list_rows[pl.ds(step, 1), :] == row_ids, 1.0, 0.0)
                    start = pl.multiple_of(step * chunk, chunk)
                    values = updates[pl.ds(start, chunk), :]
                    return total + jnp.dot(ones.astype(BF16), values, preferred_element_type=F32)

                return lax.fori_loop(
                    first_chunk, list_rows.shape[0], one, jnp.zeros((rows, columns), F32),
                    unroll=True,
                )

            total = reduce_blocks(depth, reducing, scattered)
            combined = (total + rhs[depth][...].astype(F32)).astype(BF16)
        else:
            combined = rhs[depth][...]
        block_of(full, mine)[...] = combined
        sums = [None]
        ready = [False]

        def multiply(index, depth=depth, full=full, sums=sums, ready=ready):
            if not streamed:
                return
            if not ready[0]:
                wait_factor(depth)
                ready[0] = True
            part = row_parts(inv[depth], aligned(index * rows), rows)
            block = block_of(full, index)[...]
            terms = [jnp.dot(value, block, preferred_element_type=F32) for value in part]
            old = sums[0]
            sums[0] = terms if old is None else [a + b for a, b in zip(old, terms)]

        gather_blocks(depth, gathering, multiply)
        if not streamed:
            wait_factor(depth)
            part = row_parts(inv[depth], 0, sizes[depth])
            sums[0] = [jnp.dot(value, full[...], preferred_element_type=F32) for value in part]
        values = [value.astype(BF16) for value in sums[0]]
        write_values(forwards[depth], values)
        if depth:
            wait_factor(LEVELS + depth)

            def update_chunk(step, carry, depth=depth, values=values):
                start = pl.multiple_of(step * chunk, chunk)
                place = pl.multiple_of(places[depth] + step * chunk, chunk)
                values = read_values(forwards[depth])
                updates[pl.ds(place, chunk), :] = contracted(
                    coup[depth], start, chunk, values
                ).astype(BF16)
                return carry

            lax.fori_loop(0, sizes[depth] // chunk, update_chunk, 0, unroll=True)

    picked[...] = jnp.zeros_like(picked)
    for depth in range(LEVELS):
        groups = leaf_count >> depth
        mine = lax.rem(me, groups)
        reducing, gathering = levels_backward[depth]
        if depth:
            def pull(step, totals, depth=depth):
                start = pl.multiple_of(step * chunk, chunk)
                place = pl.multiple_of(places[depth] + step * chunk, chunk)
                part = row_parts(coup[depth], start, chunk)
                rows_now = picked[pl.ds(place, chunk), :].astype(BF16)
                return [
                    total - jnp.dot(value, rows_now, preferred_element_type=F32)
                    for total, value in zip(totals, part)
                ]

            totals = [value.astype(F32) for value in read_values(forwards[depth])]
            totals = lax.fori_loop(0, sizes[depth] // chunk, pull, totals, unroll=True)
            write_values(forwards[depth], [value.astype(BF16) for value in totals])

        if streamed:
            def product(index, depth=depth):
                values = read_values(forwards[depth])
                return contracted(inv[depth], aligned(index * rows), rows, values)
        else:
            whole_product = reducing[0]
            values = read_values(forwards[depth])
            whole_product[...] = contracted(inv[depth], 0, sizes[depth], values).astype(BF16)

            def product(index, whole_product=whole_product):
                return block_of(whole_product, index)[...].astype(F32)

        solved = reduce_blocks(depth, reducing, product).astype(BF16)
        outs[depth][...] = solved
        if gathering is not None:
            full = gathering[0]
            block_of(full, mine)[...] = solved
            first_chunk = places[depth + 1] // chunk

            def pick(index, depth=depth, full=full, first_chunk=first_chunk):
                base = offsets[depth] + index * rows
                row_ids = lax.broadcasted_iota(jnp.int32, (chunk, rows), 1) + base
                block = block_of(full, index)[...]

                def one(step, carry):
                    start = pl.multiple_of(step * chunk, chunk)
                    here = pl.ds(start, chunk)
                    ones = jnp.where(list_cols[here, :] == row_ids, 1.0, 0.0).astype(BF16)
                    picked[here, :] += jnp.dot(ones, block, preferred_element_type=F32)
                    return carry

                lax.fori_loop(first_chunk, list_rows.shape[0], one, 0, unroll=True)

            gather_blocks(depth, gathering, pick)

    for copy in late:
        copy.wait_send()
    for factor in factors:
        for shift in range(1, panel_count):
            remote_factor(*factor, shift).wait_send()


def body(*args):
    rhs, inv, coup, lists = args[:4], args[4:8], args[8:11], args[11:]
    rows, columns = rhs[0].shape
    leaf_count = lax.axis_size("leaf")
    panel_count = lax.axis_size("panel")
    factor_rows = inv[0].shape[0]
    sizes = [value.shape[1] for value in inv]
    chunk = sizes[-1]
    leaf = lax.axis_index("leaf")
    chosen = []
    for depth in range(1, LEVELS):
        front = leaf // (leaf_count >> depth)
        chosen.append(lax.dynamic_index_in_dim(lists[depth - 1], front, 0, keepdims=False))
    joined = jnp.concatenate(chosen)
    list_rows = joined.reshape(-1, chunk)
    list_cols = joined.reshape(-1, 1)
    dma = pltpu.SemaphoreType.DMA
    vmem = pltpu.VMEM
    scratch = [vmem((panel_count, factor_rows, size), BF16) for size in sizes]
    scratch += [vmem((panel_count, factor_rows, size), BF16) for size in sizes[1:]]
    scratch += [vmem((panel_count, factor_rows, columns), BF16) for _ in sizes]
    scratch += [vmem((joined.shape[0], columns), BF16), vmem((joined.shape[0], columns), F32)]
    peers = max(panel_count - 1, 1)
    scratch += [dma((2 * LEVELS,)), dma((2 * LEVELS, peers)), dma((2 * LEVELS, peers))]

    def reduce_scratch(depth):
        low, high = split_group(leaf_count >> depth)
        highs = max(high - 1, 1)
        lows = max(low - 1, 1)
        return [
            vmem((sizes[depth], columns), BF16),
            vmem((high, rows, columns), F32),
            vmem((high, lows, rows, columns), BF16),
            vmem((highs, rows, columns), BF16),
            vmem((highs, rows, columns), BF16),
            dma((high, lows)), dma((high, lows)), dma((highs,)), dma((highs,)),
        ]

    def gather_scratch(depth):
        low, high = split_group(leaf_count >> depth)
        highs = max(high - 1, 1)
        lows = max(low - 1, 1)
        return [
            vmem((sizes[depth], columns), BF16),
            dma((high, lows)), dma((high, lows)), dma((highs,)), dma((highs,)),
        ]

    for depth in range(LEVELS):
        if depth < LEVELS - 1:
            scratch += reduce_scratch(depth)
        scratch += gather_scratch(depth)
        scratch += reduce_scratch(depth)
        if depth < LEVELS - 1:
            scratch += gather_scratch(depth)

    in_vmem = pl.BlockSpec(memory_space=vmem)
    anywhere = pl.BlockSpec(memory_space=pltpu.HBM)
    own = jax.ShapeDtypeStruct((rows, columns), BF16)
    return pl.pallas_call(
        functools.partial(kernel, leaf_count, panel_count),
        out_shape=(own,) * LEVELS,
        in_specs=[in_vmem] * LEVELS + [anywhere] * (2 * LEVELS - 1) + [in_vmem] * 2,
        out_specs=(in_vmem,) * LEVELS,
        scratch_shapes=scratch,
        compiler_params=pltpu.CompilerParams(
            collective_id=0, has_side_effects=True, vmem_limit_bytes=48 * 2**20
        ),
    )(*rhs, *inv, *coup, list_rows, list_cols)


def solution(mesh):
    in_specs = (P("leaf", "panel"),) * 4 + (P(("leaf", "panel"), None),) * 7 + (P(),) * 3
    out_specs = (P("leaf", "panel"),) * 4
    return jax.shard_map(body, mesh=mesh, in_specs=in_specs, out_specs=out_specs, check_vma=False)
```
